128 devices in a mesh: lo: 4 (over x), hi: 32 (over z, y, core).
Axes of the slice: x: 4, y: 4, z: 4, core: 2. Of those that a mesh axis runs over, the one named last changes fastest.
Arguments:
- children: float32 [8192, 64, 128], P(('lo', 'hi')), may hold values from -6 to 6
- parents: float32 [8192, 64, 128], P(('lo', 'hi')), may hold values from -6 to 6
- hamiltonian: float32 [64, 64], replicated
- damping: float32 [64], replicated, may hold values from 0.2 to 2
- coupling_real: float32 [64], replicated, may hold values from 0.3 to 2
- coupling_imag: float32 [64], replicated, may hold values from -1.5 to -0.2
- child_modes: int32 [8192, 4], P(('lo', 'hi')), may hold values from 0 to 63, as said below
- child_source: int32 [8192, 4], P(('lo', 'hi')), may hold values from 0 to 319, as said below
- parent_modes: int32 [8192, 3], P(('lo', 'hi')), may hold values from 0 to 63, as said below
- send_rows: int32 [128, 128, 2], P(('lo', 'hi')), may hold values from 0 to 63
- live_count: int32 [128], P(('lo', 'hi')), may hold values from 8 to 64, as said below
Outputs:
- child_rates: float32 [8192, 64, 128], P(('lo', 'hi'))
- parent_rates: float32 [8192, 64, 128], P(('lo', 'hi'))
The draws below stay inside these ranges and needn't reach their ends.
Inputs may be any that keep to these rules, and one draw needn't show every extreme that they name: `child_modes`: the four modes of a row are distinct. `parent_modes`: the three modes of a row are distinct. `child_source`: the slots of one device name at most 4 times values q >= 64 with one and the same e = (q - 64) // 2; on every device some e is named exactly 4 times. `live_count`: some device is full and some holds 8 live matrices.
All inputs are finite; a program needn't handle non-finite values.
Results may differ from the reference program's by a relative error of at most 0.0003.
Values sent between devices are 32-bit elements; how exact they have to be, the bound alone decides.
A program may use at most 192 MiB of HBM per device.

```python
import math
import jax
import jax.numpy as jnp
from jax import lax

PIGMENTS = 64
SLAB_DEV = 64
PARENTS_DEV = 64
CAPACITY = 2
REQUESTS = 4
SLAB = 8192
SECTION = 8192
DEVICES = 128


def draw_hamiltonian(key, part):
    first, second = jax.random.split(key)
    raw = jax.random.normal(first, (PIGMENTS, PIGMENTS), jnp.float32)
    energies = jax.random.uniform(second, (PIGMENTS,), jnp.float32, -1.0, 1.0)
    return 0.5 * (raw + raw.T) / jnp.sqrt(1.0 * PIGMENTS) + jnp.diag(energies)


def draw_child_modes(key, part):
    first, second = jax.random.split(key)
    base = jax.random.randint(first, (SLAB, 1), 0, PIGMENTS)
    quarter = PIGMENTS // 4
    offsets = jax.random.randint(second, (SLAB, 3), 0, quarter) + jnp.array([1, 2, 3], jnp.int32)[None, :] * quarter
    return jnp.concatenate([base, (base + offsets) % PIGMENTS], axis=1).astype(jnp.int32)


def draw_parent_modes(key, part):
    first, second = jax.random.split(key)
    base = jax.random.randint(first, (SECTION, 1), 0, PIGMENTS)
    third = PIGMENTS // 3
    offsets = jax.random.randint(second, (SECTION, 2), 0, third) + jnp.array([1, 2], jnp.int32)[None, :] * third
    return jnp.concatenate([base, (base + offsets) % PIGMENTS], axis=1).astype(jnp.int32)


def draw_child_source(key, part):
    first, second, third, fourth = jax.random.split(key, 4)
    slot_count = SLAB_DEV * 4
    candidates = DEVICES * REQUESTS
    local = jax.random.randint(first, (DEVICES, slot_count), 0, PARENTS_DEV)
    coin = jax.random.randint(second, (DEVICES, slot_count), 0, 2)
    forced = jnp.arange(slot_count, dtype=jnp.int32) < REQUESTS
    remote_flag = (coin == 1) | forced[None, :]
    rank = jnp.cumsum(remote_flag.astype(jnp.int32), axis=1) - 1
    keys = jax.random.split(third, DEVICES)

    def order_of(device_key):
        shuffled = jax.random.permutation(device_key, candidates)
        owners = (shuffled // REQUESTS).astype(jnp.int32)
        score = jnp.where(owners == owners[0], -1, jnp.arange(candidates, dtype=jnp.int32))
        return owners[jnp.argsort(score, stable=True)]
    ordered = jax.vmap(order_of)(keys)
    owner = jnp.take_along_axis(ordered, jnp.clip(rank, 0, candidates - 1), axis=1)
    place = jax.random.randint(fourth, (DEVICES, slot_count), 0, CAPACITY)
    usable = remote_flag & (rank < candidates)
    source = jnp.where(usable, PARENTS_DEV + owner * CAPACITY + place, local)
    return source.reshape(SLAB, 4).astype(jnp.int32)


def draw_live_count(key, part):
    first, second, third = jax.random.split(key, 3)
    counts = jax.random.randint(first, (DEVICES,), SLAB_DEV // 8, SLAB_DEV + 1)
    fullest = jax.random.randint(second, (), 0, DEVICES)
    emptiest = (fullest + 1 + jax.random.randint(third, (), 0, DEVICES - 1)) % DEVICES
    places = jnp.arange(DEVICES, dtype=jnp.int32)
    counts = jnp.where(places == fullest, SLAB_DEV, counts)
    counts = jnp.where(places == emptiest, SLAB_DEV // 8, counts)
    return counts.astype(jnp.int32)


def place_ends(result, own_key, smallest, high):
    longest = result.shape.index(max(result.shape))
    spots = []
    for shift in (0, 1):
        where = [jax.random.randint(jax.random.fold_in(own_key, axis), (), 0, length) for axis, length in enumerate(result.shape)]
        where[longest] = (where[longest] + shift) % result.shape[longest]
        spots.append(tuple(where))
    return result.at[spots[0]].set(smallest).at[spots[1]].set(high)


def shard_levels(own_key, extent, pieces, least, high):
    level, own = 1.0, jax.random.fold_in(own_key, 6)
    for dim, shards_of in pieces:
        draws = jnp.exp(jax.random.uniform(jax.random.fold_in(own, dim), (shards_of,), jnp.float32, least / len(pieces), high / len(pieces)))
        level = level * jnp.repeat(draws, extent[dim] // shards_of).reshape([-1 if axis == dim else 1 for axis in range(len(extent))])
    return level


def noise(rng, dims, spread, bound, pieces=(), held_as=jnp.bfloat16):
    factor_of = shard_levels(rng, dims, pieces, -0.22, 0.18) if pieces else 1.0
    result = jax.random.normal(rng, dims, jnp.float32) * spread * factor_of
    return jnp.minimum(jnp.maximum(result, -bound), bound).astype(held_as)


def setup_inputs(seed: int = 0) -> dict:
    key_list = jax.random.split(jax.random.key(seed), 12)
    return {
        "children": noise(key_list[0], (SLAB, PIGMENTS, 2 * PIGMENTS), 1.0, 6.0, ((0, 128),), jnp.float32),
        "parents": noise(key_list[1], (SECTION, PIGMENTS, 2 * PIGMENTS), 1.0, 6.0, ((0, 128),), jnp.float32),
        "hamiltonian": draw_hamiltonian(jax.random.fold_in(key_list[11], 71), 0),
        "damping": jnp.clip(jnp.exp(jax.random.uniform(key_list[3], (PIGMENTS,), jnp.float32, math.log(0.2), math.log(2.0))), 0.2, 2.0),
        "coupling_real": jnp.clip(jnp.exp(jax.random.uniform(key_list[4], (PIGMENTS,), jnp.float32, math.log(0.3), math.log(2.0))), 0.3, 2.0),
        "coupling_imag": jnp.clip(jax.random.uniform(key_list[5], (PIGMENTS,), jnp.float32, -1.5, -0.2), -1.5, -0.2),
        "child_modes": draw_child_modes(jax.random.fold_in(key_list[11], 71), 0),
        "child_source": draw_child_source(jax.random.fold_in(key_list[11], 71), 0),
        "parent_modes": draw_parent_modes(jax.random.fold_in(key_list[11], 71), 0),
        "send_rows": place_ends(jax.random.randint(key_list[9], (DEVICES, DEVICES, CAPACITY), 0, PARENTS_DEV), jax.random.fold_in(key_list[9], 1), 0, PARENTS_DEV - 1).astype(jnp.int32),
        "live_count": draw_live_count(jax.random.fold_in(key_list[11], 71), 0),
    }


HIGHEST = lax.Precision.HIGHEST


def select_modes(modes, pigments):
    return (modes[:, None] == jnp.arange(pigments, dtype=jnp.int32)[None, :]).astype(jnp.float32)


def commute(matrices, hamiltonian):
    pigments = hamiltonian.shape[0]
    left_side = jnp.einsum('rs,asc->arc', hamiltonian, matrices, precision=HIGHEST)
    quarters = matrices.reshape(matrices.shape[0], pigments, 2, pigments)
    right_side = jnp.einsum('arpc,cd->arpd', quarters, hamiltonian, precision=HIGHEST).reshape(matrices.shape)
    difference = left_side - right_side
    return jnp.concatenate([difference[..., pigments:], -difference[..., :pigments]], axis=-1)


def assemble(onehot, row_real, row_imag, col_real, col_imag):
    part_real = onehot[:, :, None] * row_real[:, None, :] - col_real[:, :, None] * onehot[:, None, :]
    part_imag = onehot[:, :, None] * row_imag[:, None, :] - col_imag[:, :, None] * onehot[:, None, :]
    return jnp.concatenate([part_imag, -part_real], axis=-1)


def row_and_column(matrices, onehot):
    pigments = onehot.shape[1]
    picked_row = jnp.einsum('ar,arc->ac', onehot, matrices, precision=HIGHEST)
    col_real = jnp.einsum('arc,ac->ar', matrices[..., :pigments], onehot, precision=HIGHEST)
    col_imag = jnp.einsum('arc,ac->ar', matrices[..., pigments:], onehot, precision=HIGHEST)
    return picked_row[:, :pigments], picked_row[:, pigments:], col_real, col_imag


def raise_term(matrices, onehot):
    row_real, row_imag, col_real, col_imag = row_and_column(matrices, onehot)
    return assemble(onehot, row_real, row_imag, col_real, col_imag)


def lower_term(matrices, onehot, coupling_real, coupling_imag):
    row_real, row_imag, col_real, col_imag = row_and_column(matrices, onehot)
    factor_real = jnp.dot(onehot, coupling_real, precision=HIGHEST)[:, None]
    factor_imag = jnp.dot(onehot, coupling_imag, precision=HIGHEST)[:, None]
    return assemble(onehot,
                    factor_real * row_real - factor_imag * row_imag,
                    factor_real * row_imag + factor_imag * row_real,
                    factor_real * col_real + factor_imag * col_imag,
                    factor_real * col_imag - factor_imag * col_real)


def damping_sum(modes, damping, pigments):
    counts = select_modes(modes[:, 0], pigments)
    for place in range(1, modes.shape[1]):
        counts = counts + select_modes(modes[:, place], pigments)
    return jnp.dot(counts, damping, precision=HIGHEST)


def reference(children, parents, hamiltonian, damping, coupling_real, coupling_imag, child_modes, child_source, parent_modes, send_rows, live_count):
    pigments = hamiltonian.shape[0]
    devices = live_count.shape[0]
    slab_dev = children.shape[0] // devices
    parents_dev = parents.shape[0] // devices
    capacity = send_rows.shape[2]

    def one_device(totals, item):
        device, matrices, modes, source, live = item
        remote = jnp.maximum(source - parents_dev, 0)
        peer = remote // capacity
        place = remote % capacity
        remote_index = peer * parents_dev + send_rows[peer, device, place]
        local_index = device * parents_dev + source
        parent_of = jnp.where(source < parents_dev, local_index, remote_index).astype(jnp.int32)
        alive = (jnp.arange(slab_dev, dtype=jnp.int32) < live).astype(jnp.float32)
        rates = commute(matrices, hamiltonian) - damping_sum(modes, damping, pigments)[:, None, None] * matrices
        for slot in range(4):
            onehot = select_modes(modes[:, slot], pigments)
            picked = parents[parent_of[:, slot]]
            rates = rates + lower_term(picked, onehot, coupling_real, coupling_imag)
            totals = totals.at[parent_of[:, slot]].add(raise_term(matrices, onehot) * alive[:, None, None])
        return totals, rates * alive[:, None, None]

    start = jnp.zeros(parents.shape, jnp.float32)
    items = (jnp.arange(devices, dtype=jnp.int32),
             children.reshape(devices, slab_dev, pigments, 2 * pigments),
             child_modes.reshape(devices, slab_dev, 4),
             child_source.reshape(devices, slab_dev, 4),
             live_count)
    totals, rates = lax.scan(one_device, start, items)
    parent_rates = commute(parents, hamiltonian) - damping_sum(parent_modes, damping, pigments)[:, None, None] * parents + totals
    return rates.reshape(children.shape), parent_rates
```

```python
import jax
import jax.numpy as jnp
from jax import lax
from jax.experimental import pallas as pl
from jax.experimental.pallas import tpu as pltpu
from jax.sharding import PartitionSpec as P

MESH = pl.DeviceIdType.MESH
F32 = jnp.float32
BF16 = jnp.bfloat16
I32 = jnp.int32
LANES = 128
HALF = 64
ROWS = 4096
SLOTS = 256
PLACES = 4
CHUNK = 256
DEVICES = 128
BOX = DEVICES * 2 * PLACES
REQS = DEVICES * PLACES


def iota(shape, axis):
    return lax.broadcasted_iota(I32, shape, axis)


def split(x):
    high = x.astype(BF16)
    return high, (x - high.astype(F32)).astype(BF16)


def side_by_side(x):
    return jnp.concatenate(split(x), axis=1)


def dot(a, b):
    return lax.dot_general(a, b, (((1,), (0,)), ((), ())), preferred_element_type=F32)


def dot_nt(a, b):
    return lax.dot_general(a, b, (((1,), (1,)), ((), ())), preferred_element_type=F32)


def turn(x):
    return pltpu.roll(x, HALF, 1)


def rearrange(flipped):
    left = iota((HALF, LANES), 1) < HALF
    blocks = []
    for pair in range(2):
        top = flipped[:HALF, pair * LANES : (pair + 1) * LANES]
        low = flipped[HALF:, pair * LANES : (pair + 1) * LANES]
        blocks.append(jnp.where(left, top, turn(low)))
        blocks.append(jnp.where(left, turn(top), low))
    return jnp.concatenate(blocks, axis=0)


def transposed_chunk(x):
    eye = (iota((LANES, 2 * LANES), 0) == lax.rem(iota((LANES, 2 * LANES), 1), LANES)).astype(F32).astype(BF16)
    return rearrange(dot_nt(eye, side_by_side(x)))


def column(table):
    return jnp.concatenate([table[:, s : s + 1] for s in range(4)], axis=0)


def as_row(col):
    return jnp.broadcast_to(col.astype(F32), (col.shape[0], LANES)).T[0:1, :].astype(I32)


def slot_places(source):
    q_col = column(source)
    q_row = as_row(q_col)
    far_col, far_row = q_col >= HALF, q_row >= HALF
    owner_col = jnp.where(far_col, (q_col - HALF) >> 1, -1)
    owner_row = jnp.where(far_row, (q_row - HALF) >> 1, -1)
    same = (owner_col == owner_row).astype(I32)
    down, across = iota((SLOTS, SLOTS), 0), iota((SLOTS, SLOTS), 1)
    before = jnp.where(across < down, same, 0).astype(F32)
    after = jnp.where(down < across, same, 0).astype(F32)
    rank_col = jnp.sum(before, axis=1, keepdims=True).astype(I32)
    rank_row = jnp.sum(after, axis=0, keepdims=True).astype(I32)
    return owner_col, rank_col, owner_row, rank_row


def exchange_kernel(
    modes_s, source_s, live_s, modes, source, table, children, parents,
    inbox, answers, raised_row, raised_col, near_row, near_col,
    kids, kids_t, folks, folks_t, outbox, reply, targets, targets_s,
    in_sem, local_sem, send_sem, recv_sem,
):
    lo, hi = lax.axis_index("lo"), lax.axis_index("hi")
    me = lo * 32 + hi
    get_kids = pltpu.make_async_copy(children, kids, in_sem.at[0])
    get_folks = pltpu.make_async_copy(parents, folks, in_sem.at[1])
    get_kids.start()
    get_folks.start()

    barrier = pltpu.get_barrier_semaphore()

    def greet(k, carry):
        peer = lax.rem(me + k, DEVICES)
        pl.semaphore_signal(barrier, 1, device_id=(peer // 32, lax.rem(peer, 32)), device_id_type=MESH)
        return carry

    lax.fori_loop(1, DEVICES, greet, 0)

    owner_col, rank_col, owner_row, rank_row = slot_places(source[...])
    mode_col = column(modes[...])
    q_col = column(source[...])
    place_col = lax.rem(jnp.maximum(q_col - HALF, 0), 2)
    alive_col = (lax.rem(iota((SLOTS, 1), 0), HALF) < live_s[0])

    get_kids.wait()

    def turn_kids(i, carry):
        at = pl.ds(pl.multiple_of(i * CHUNK, CHUNK), CHUNK)
        kids_t[at, :] = transposed_chunk(kids[at, :])
        return carry

    lax.fori_loop(0, ROWS // CHUNK, turn_kids, 0)

    def pick_kids(a, carry):
        for s in range(4):
            line = a * HALF + modes_s[a, s]
            raised_row[pl.ds(s * HALF + a, 1), :] = kids[pl.ds(line, 1), :]
            raised_col[pl.ds(s * HALF + a, 1), :] = kids_t[pl.ds(line, 1), :]
        return carry

    lax.fori_loop(0, HALF, pick_kids, 0, unroll=4)

    lane = iota((SLOTS, LANES), 1)
    diagonal = lax.rem(lane, HALF) == mode_col
    gone = diagonal | jnp.logical_not(alive_col)
    row = jnp.where(gone, 0.0, raised_row[...])
    col = jnp.where(gone, 0.0, raised_col[...])
    raised_row[...] = row
    raised_col[...] = col
    code = (place_col * HALF + mode_col + 1).astype(F32)
    sent = jnp.where(lane == mode_col, col[:, 0:1], col)
    sent = jnp.where(lane == 0, code, sent)
    spot_row = jnp.where(owner_row >= 0, rank_row * DEVICES + owner_row, -1)
    pick = (iota((REQS, SLOTS), 0) == spot_row).astype(F32).astype(BF16)
    row_high, row_low = split(row)
    col_high, col_low = split(sent)
    packed = dot(pick, jnp.concatenate([row_high, col_high, row_low, col_low], axis=1))
    packed = packed[:, : 2 * LANES] + packed[:, 2 * LANES :]
    for j in range(PLACES):
        part = packed[j * DEVICES : (j + 1) * DEVICES]
        outbox[pl.ds(j, DEVICES, stride=8), :] = part[:, :LANES]
        outbox[pl.ds(PLACES + j, DEVICES, stride=8), :] = part[:, LANES:]

    pl.semaphore_wait(barrier, DEVICES - 1)

    def tile(ref, d):
        return ref.at[pl.ds(pl.multiple_of(d * 8, 8), 8), :]

    def send_all(src, dst, which):
        own = pltpu.make_async_copy(tile(src, me), tile(dst, me), local_sem.at[which])
        own.start()

        def send(k, carry):
            peer = lax.rem(me + k, DEVICES)
            pltpu.make_async_remote_copy(
                src_ref=tile(src, peer),
                dst_ref=tile(dst, me),
                send_sem=send_sem.at[which],
                recv_sem=recv_sem.at[which],
                device_id=(peer // 32, lax.rem(peer, 32)),
                device_id_type=MESH,
            ).start()
            return carry

        lax.fori_loop(1, DEVICES, send, 0)
        return own

    def wait_all(own, src, dst, sem):
        whole = pl.ds(0, BOX - 8)
        if own is not None:
            own.wait()
        pltpu.make_async_copy(src.at[whole, :], dst.at[whole, :], sem).wait()

    own = send_all(outbox, inbox, 0)

    get_folks.wait()

    def turn_folks(i, carry):
        at = pl.ds(pl.multiple_of(i * CHUNK, CHUNK), CHUNK)
        folks_t[at, :] = transposed_chunk(folks[at, :])
        return carry

    lax.fori_loop(0, ROWS // CHUNK, turn_folks, 0)

    def pick_near(a, carry):
        for s in range(4):
            q = source_s[a, s]
            line = jnp.minimum(q, HALF - 1) * HALF + modes_s[a, s]
            near_row[pl.ds(s * HALF + a, 1), :] = folks[pl.ds(line, 1), :]
            near_col[pl.ds(s * HALF + a, 1), :] = folks_t[pl.ds(line, 1), :]
        return carry

    lax.fori_loop(0, HALF, pick_near, 0, unroll=4)

    wait_all(own, outbox, inbox, recv_sem.at[0])

    wanted = jnp.zeros((DEVICES, LANES), F32)
    across = iota((DEVICES, LANES), 1)
    for j in range(PLACES):
        line = request_line(inbox[pl.ds(PLACES + j, DEVICES, stride=8), :], table[...])
        wanted = jnp.where(across == j, line.astype(F32), wanted)
    targets[...] = jnp.clip(wanted.T[:8, :].astype(I32), 0, ROWS - 1)
    to_scalar = pltpu.make_async_copy(targets, targets_s, in_sem.at[2])
    to_scalar.start()
    to_scalar.wait()

    def answer(d, carry):
        for j in range(PLACES):
            line = targets_s[j, d]
            reply[pl.ds(d * 8 + j, 1), :] = folks[pl.ds(line, 1), :]
            reply[pl.ds(d * 8 + PLACES + j, 1), :] = folks_t[pl.ds(line, 1), :]
        return carry

    lax.fori_loop(0, DEVICES, answer, 0, unroll=4)
    own = send_all(reply, answers, 1)
    wait_all(None, outbox, inbox, send_sem.at[0])
    wait_all(own, reply, answers, recv_sem.at[1])
    wait_all(None, reply, answers, send_sem.at[1])


def request_line(col, table):
    code = col[:, 0:1].astype(I32)
    wanted = jnp.clip(code - 1, 0, 2 * HALF - 1)
    chosen = jnp.where(wanted >= HALF, table[:, 1:2], table[:, 0:1])
    return chosen * HALF + lax.rem(wanted, HALF)


def rates_kernel(
    modes_s, parent_modes_s, live_s, damping_s,
    modes, source, table, hamiltonian, couple, inbox, answers, raised_row, raised_col, near_row, near_col,
    children, parents,
    child_out, parent_out,
    weights, left, p_rows, p_cols, p_line, c_rows, c_cols, c_line,
):
    step = pl.program_id(0)

    @pl.when(step == 0)
    def _():
        prepare(
            live_s, modes, source, table, hamiltonian, couple, inbox, answers, raised_row, raised_col, near_row,
            near_col, weights, left, p_rows, p_cols, p_line, c_rows, c_cols, c_line,
        )

    base = step * CHUNK
    for x_ref, out, rows, cols, line, modes_ref, places in (
        (children, child_out, c_rows, c_cols, c_line, modes_s, 4),
        (parents, parent_out, p_rows, p_cols, p_line, parent_modes_s, 3),
    ):
        x = x_ref[...]
        both = side_by_side(x)
        right = dot(both, weights[...])
        right = right[:, :LANES] + right[:, LANES:]
        lefts = dot(left[...], both)
        lefts = lefts[:CHUNK] + lefts[CHUNK:]
        lefts = lefts[:, :LANES] + lefts[:, LANES:]
        count = line.shape[1]
        hot = (iota((CHUNK, count), 0) + base == line[...]).astype(F32).astype(BF16)
        more = dot(hot, rows[...])
        more = more[:, :LANES] + more[:, LANES:]
        less = dot_nt(cols[...], hot)
        less = rearrange(less[:LANES] + less[LANES:])
        part = turn(lefts - right + more - less)
        part = jnp.where(iota((CHUNK, LANES), 1) < HALF, part, -part)
        for k in range(4):
            a = step * 4 + k
            rate = damping_s[modes_ref[a, 0]]
            for s in range(1, places):
                rate = rate + damping_s[modes_ref[a, s]]
            at = slice(k * HALF, (k + 1) * HALF)
            result = part[at] - rate * x[at]
            if out is child_out:
                result = jnp.where(a < live_s[0], result, 0.0)
            out[at, :] = result


def prepare(
    live_s, modes, source, table, hamiltonian, couple, inbox, answers, raised_row, raised_col, near_row, near_col,
    weights, left, p_rows, p_cols, p_line, c_rows, c_cols, c_line,
):
    h = hamiltonian[...]
    wide = jnp.concatenate([h, h], axis=1)
    tall = jnp.concatenate([wide] * 4, axis=0)
    square = jnp.where(
        lax.rem(iota((2 * LANES, LANES), 0) // HALF, 2) == iota((2 * LANES, LANES), 1) // HALF, tall, 0.0
    )
    weights[...] = side_by_side(square)
    four = jnp.concatenate([tall, tall], axis=1)
    diag = jnp.where(iota((CHUNK, CHUNK), 0) // HALF == iota((CHUNK, CHUNK), 1) // HALF, four, 0.0)
    left[...] = jnp.concatenate(split(diag), axis=0)

    wanted = jnp.zeros((DEVICES, LANES), F32)
    across = iota((DEVICES, LANES), 1)
    for j in range(PLACES):
        row = inbox[pl.ds(j, DEVICES, stride=8), :]
        col = inbox[pl.ds(PLACES + j, DEVICES, stride=8), :]
        line = request_line(col, table[...])
        wanted = jnp.where(across == j, line.astype(F32), wanted)
        mode = lax.rem(line, HALF)
        hit = across == mode
        first = jnp.sum(jnp.where(hit, col, 0.0), axis=1, keepdims=True)
        first = jnp.where(mode == 0, 0.0, first)
        col = jnp.where(across == 0, first, jnp.where(hit, 0.0, col))
        put_lines(row, col, p_rows, p_cols, j * DEVICES)
    lines = wanted.T.astype(I32)
    for j in range(PLACES):
        p_line[:, j * DEVICES : (j + 1) * DEVICES] = lines[j : j + 1, :]
    mode_col, q_col = column(modes[...]), column(source[...])
    own_line = jnp.where(q_col < HALF, q_col * HALF + mode_col, ROWS)
    p_line[:, REQS:] = as_row(own_line)
    for k in range(2):
        at = slice(k * LANES, (k + 1) * LANES)
        put_lines(raised_row[at, :], raised_col[at, :], p_rows, p_cols, REQS + k * LANES)

    owner_col, rank_col, _, _ = slot_places(source[...])
    spot = jnp.where(owner_col >= 0, owner_col * 8 + rank_col, -8)
    spots = jnp.concatenate([spot, spot + PLACES], axis=0)
    pick = (iota((2 * SLOTS, BOX), 1) == spots).astype(F32).astype(BF16)
    got = dot(pick, side_by_side(answers[...]))
    got = got[:, :LANES] + got[:, LANES:]
    near = owner_col < 0
    row = jnp.where(near, near_row[...], got[:SLOTS])
    col = jnp.where(near, near_col[...], got[SLOTS:])
    lane = iota((SLOTS, LANES), 1)
    real = jnp.sum(jnp.where(lane == mode_col, couple[0:1, :], 0.0), axis=1, keepdims=True)
    imag = jnp.sum(jnp.where(lane == mode_col, couple[1:2, :], 0.0), axis=1, keepdims=True)
    signed = jnp.where(lane < HALF, -imag, imag)
    row = real * row + signed * turn(row)
    col = real * col - signed * turn(col)
    for k in range(2):
        at = slice(k * LANES, (k + 1) * LANES)
        put_lines(row[at], col[at], c_rows, c_cols, k * LANES)
    c_line[...] = as_row(lax.rem(iota((SLOTS, 1), 0), HALF) * HALF + mode_col)


def put_lines(row, col, rows, cols, at):
    rows[at : at + LANES, :] = side_by_side(row)
    cols[:, at : at + LANES] = jnp.concatenate(split(col.T), axis=0)


VMEM = pl.BlockSpec(memory_space=pltpu.VMEM)
SMEM = pl.BlockSpec(memory_space=pltpu.SMEM)
ANY = pl.BlockSpec(memory_space=pl.ANY)


def body(
    children, parents, hamiltonian, damping, coupling_real, coupling_imag,
    child_modes, child_source, parent_modes, send_rows, live_count,
):
    kids = children.reshape(ROWS, LANES)
    folks = parents.reshape(ROWS, LANES)
    table = send_rows[0]
    lines = jax.ShapeDtypeStruct((SLOTS, LANES), F32)
    box = jax.ShapeDtypeStruct((BOX, LANES), F32)
    inbox, answers, raised_row, raised_col, near_row, near_col = pl.pallas_call(
        exchange_kernel,
        out_shape=(box, box, lines, lines, lines, lines),
        in_specs=[SMEM, SMEM, SMEM, VMEM, VMEM, VMEM, ANY, ANY],
        out_specs=(VMEM,) * 6,
        scratch_shapes=[
            pltpu.VMEM((ROWS, LANES), F32),
            pltpu.VMEM((ROWS, LANES), F32),
            pltpu.VMEM((ROWS, LANES), F32),
            pltpu.VMEM((ROWS, LANES), F32),
            pltpu.VMEM((BOX, LANES), F32),
            pltpu.VMEM((BOX, LANES), F32),
            pltpu.VMEM((8, LANES), I32),
            pltpu.SMEM((8, LANES), I32),
            pltpu.SemaphoreType.DMA((3,)),
            pltpu.SemaphoreType.DMA((2,)),
            pltpu.SemaphoreType.DMA((2,)),
            pltpu.SemaphoreType.DMA((2,)),
        ],
        compiler_params=pltpu.CompilerParams(
            collective_id=0, has_side_effects=True, vmem_limit_bytes=32 * 2**20
        ),
    )(child_modes, child_source, live_count, child_modes, child_source, table, kids, folks)
    couple = jnp.concatenate(
        [jnp.stack([coupling_real, coupling_imag]), jnp.zeros((2, LANES - HALF), F32)], axis=1
    )
    chunk = pl.BlockSpec((CHUNK, LANES), lambda i: (i, 0))
    whole = jax.ShapeDtypeStruct((ROWS, LANES), F32)
    every = REQS + SLOTS
    child_rates, parent_rates = pl.pallas_call(
        rates_kernel,
        grid=(ROWS // CHUNK,),
        out_shape=(whole, whole),
        in_specs=[SMEM] * 4 + [VMEM] * 11 + [chunk] * 2,
        out_specs=(chunk, chunk),
        scratch_shapes=[
            pltpu.VMEM((2 * LANES, 2 * LANES), BF16),
            pltpu.VMEM((2 * CHUNK, CHUNK), BF16),
            pltpu.VMEM((every, 2 * LANES), BF16),
            pltpu.VMEM((2 * LANES, every), BF16),
            pltpu.VMEM((1, every), I32),
            pltpu.VMEM((SLOTS, 2 * LANES), BF16),
            pltpu.VMEM((2 * LANES, SLOTS), BF16),
            pltpu.VMEM((1, SLOTS), I32),
        ],
        compiler_params=pltpu.CompilerParams(vmem_limit_bytes=32 * 2**20),
    )(
        child_modes, parent_modes, live_count, damping,
        child_modes, child_source, table, hamiltonian, couple,
        inbox, answers, raised_row, raised_col, near_row, near_col, kids, folks,
    )
    return child_rates.reshape(children.shape), parent_rates.reshape(parents.shape)


def solution(mesh):
    in_specs = (
        P(("lo", "hi"), None, None),
        P(("lo", "hi"), None, None),
        P(),
        P(),
        P(),
        P(),
        P(("lo", "hi"), None),
        P(("lo", "hi"), None),
        P(("lo", "hi"), None),
        P(("lo", "hi"), None, None),
        P(("lo", "hi")),
    )
    out_specs = (P(("lo", "hi"), None, None), P(("lo", "hi"), None, None))
    return jax.shard_map(body, mesh=mesh, in_specs=in_specs, out_specs=out_specs, check_vma=False)
```

```python
import jax
import jax.numpy as jnp
from jax import lax
from jax.experimental import pallas as pl
from jax.experimental.pallas import tpu as pltpu
from jax.sharding import PartitionSpec as P

MESH = pl.DeviceIdType.MESH
F32 = jnp.float32
BF16 = jnp.bfloat16
I32 = jnp.int32
LANES = 128
HALF = 64
ROWS = 4096
SLOTS = 256
PLACES = 4
CHUNK = 256
DEVICES = 128
STRIDE = 43
BOX = DEVICES * 2 * PLACES
REQS = DEVICES * PLACES


def iota(shape, axis):
    return lax.broadcasted_iota(I32, shape, axis)


def split(x):
    high = x.astype(BF16)
    return high, (x - high.astype(F32)).astype(BF16)


def side_by_side(x):
    return jnp.concatenate(split(x), axis=1)


def dot(a, b):
    return lax.dot_general(a, b, (((1,), (0,)), ((), ())), preferred_element_type=F32)


def dot_nt(a, b):
    return lax.dot_general(a, b, (((1,), (1,)), ((), ())), preferred_element_type=F32)


def turn(x):
    return pltpu.roll(x, HALF, 1)


def rearrange(flipped):
    left = iota((HALF, LANES), 1) < HALF
    blocks = []
    for pair in range(2):
        top = flipped[:HALF, pair * LANES : (pair + 1) * LANES]
        low = flipped[HALF:, pair * LANES : (pair + 1) * LANES]
        blocks.append(jnp.where(left, top, turn(low)))
        blocks.append(jnp.where(left, turn(top), low))
    return jnp.concatenate(blocks, axis=0)


def transposed_chunk(both):
    eye = (iota((LANES, 2 * LANES), 0) == lax.rem(iota((LANES, 2 * LANES), 1), LANES)).astype(F32).astype(BF16)
    return rearrange(dot_nt(eye, both))


def slots_row(table):
    twice = jnp.concatenate([table, table], axis=1)
    left = iota((1, LANES), 1) < HALF
    return jnp.concatenate([jnp.where(left, twice[s : s + 1], twice[s + 1 : s + 2]) for s in (0, 2)], axis=1)


def as_column(row):
    wide = jnp.broadcast_to(row.astype(F32), (LANES, row.shape[1]))
    parts = [wide[:, k : k + LANES].T for k in range(0, row.shape[1], LANES)]
    return jnp.concatenate(parts, axis=0)[:, 0:1].astype(I32)


def as_row(col):
    return jnp.broadcast_to(col.astype(F32), (col.shape[0], LANES)).T[0:1, :].astype(I32)


def slot_places(q_row, q_col):
    owner_col = jnp.where(q_col >= HALF, (q_col - HALF) >> 1, -1)
    owner_row = jnp.where(q_row >= HALF, (q_row - HALF) >> 1, -1)
    same = (owner_col == owner_row).astype(I32)
    down, across = iota((SLOTS, SLOTS), 0), iota((SLOTS, SLOTS), 1)
    before = jnp.where(across < down, same, 0).astype(F32)
    after = jnp.where(down < across, same, 0).astype(F32)
    rank_col = jnp.sum(before, axis=1, keepdims=True).astype(I32)
    rank_row = jnp.sum(after, axis=0, keepdims=True).astype(I32)
    return owner_col, rank_col, owner_row, rank_row


def times_minus_i(x):
    y = turn(x)
    return jnp.where(iota(x.shape, 1) < HALF, y, -y)


def prepare_hamiltonian(hamiltonian, weights, left):
    h = hamiltonian[...]
    wide = jnp.concatenate([h, h], axis=1)
    tall = jnp.concatenate([wide] * 4, axis=0)
    down, across = iota((2 * LANES, LANES), 0), iota((2 * LANES, LANES), 1)
    lower = lax.rem(down // HALF, 2) == 1
    square = jnp.where(lower == (across < HALF), jnp.where(lower, tall, -tall), 0.0)
    weights[...] = side_by_side(square)
    high, low = split(wide)
    left[...] = jnp.concatenate([high, low], axis=1)


def own_terms(x, both, first, weights, left, damping_s, modes_s, places):
    right = dot(both, weights[...])
    right = right[:, :LANES] + right[:, LANES:]
    lefts = []
    for pair in range(2):
        a, b = (both[(2 * pair + n) * HALF : (2 * pair + n + 1) * HALF] for n in range(2))
        a = jnp.concatenate([a[:, :LANES], a[:, LANES:]], axis=0)
        b = jnp.concatenate([b[:, :LANES], b[:, LANES:]], axis=0)
        ab = jnp.concatenate([a, b], axis=1)
        product = dot(left[...], jnp.concatenate([ab, ab], axis=0))
        lefts += [product[:, :LANES], product[:, LANES:]]
    part = times_minus_i(jnp.concatenate(lefts, axis=0)) - right
    results = []
    for k in range(4):
        rate = damping_s[modes_s[0, first + k]]
        for s in range(1, places):
            rate = rate + damping_s[modes_s[s, first + k]]
        at = slice(k * HALF, (k + 1) * HALF)
        results.append(part[at] - rate * x[at])
    return jnp.concatenate(results, axis=0)


def slot_sums(rows, cols, line, base):
    hot = (iota((CHUNK, line.shape[1]), 0) + base == line[...]).astype(F32).astype(BF16)
    more = dot(hot, rows[...])
    less = dot_nt(cols[...], hot)
    return more[:, :LANES] + more[:, LANES:] + rearrange(less[:LANES] + less[LANES:])


def put_lines(row, col, rows, cols, at):
    rows[at : at + LANES, :] = side_by_side(times_minus_i(row))
    cols[:, at : at + LANES] = jnp.concatenate(split(-times_minus_i(col).T), axis=0)


def exchange_kernel(
    modes_s, source_s, parent_modes_s, live_s, damping_s, modes, source, table, hamiltonian, children, parents,
    answers, near_row, near_col, kids_out, folks_out,
    kids, kids_t, folks, folks_t, kids_part, folks_done, outbox, inbox, reply, raised_row, raised_col, targets, targets_s,
    weights, left, rows, cols, lines,
    in_sem, out_sem, local_sem, send_sem, recv_sem,
):
    lo, hi = lax.axis_index("lo"), lax.axis_index("hi")
    me = lo * 32 + hi
    get_kids = pltpu.make_async_copy(children, kids, in_sem.at[0])
    get_folks = pltpu.make_async_copy(parents, folks, in_sem.at[1])
    get_kids.start()
    get_folks.start()

    barrier = pltpu.get_barrier_semaphore()

    def greet(k, carry):
        peer = lax.rem(me + k, DEVICES)
        pl.semaphore_signal(barrier, 1, device_id=(peer // 32, lax.rem(peer, 32)), device_id_type=MESH)
        return carry

    lax.fori_loop(1, DEVICES, greet, 0)

    q_row, mode_row = slots_row(source[...]), slots_row(modes[...])
    q_col, mode_col = as_column(q_row), as_column(mode_row)
    _, _, owner_row, rank_row = slot_places(q_row, q_col)
    place_col = lax.rem(jnp.maximum(q_col - HALF, 0), 2)
    alive_col = lax.rem(iota((SLOTS, 1), 0), HALF) < live_s[0]

    get_kids.wait()

    def turn_kids(i, carry):
        at = pl.ds(pl.multiple_of(i * CHUNK, CHUNK), CHUNK)
        kids_t[at, :] = transposed_chunk(side_by_side(kids[at, :]))
        return carry

    lax.fori_loop(0, ROWS // CHUNK, turn_kids, 0, unroll=2)

    def pick_kids(a, carry):
        for s in range(4):
            line = a * HALF + modes_s[s, a]
            raised_row[pl.ds(s * HALF + a, 1), :] = kids[pl.ds(line, 1), :]
            raised_col[pl.ds(s * HALF + a, 1), :] = kids_t[pl.ds(line, 1), :]
        return carry

    lax.fori_loop(0, HALF, pick_kids, 0, unroll=4)

    lane = iota((SLOTS, LANES), 1)
    diagonal = lax.rem(lane, HALF) == mode_col
    gone = diagonal | jnp.logical_not(alive_col)
    row = jnp.where(gone, 0.0, raised_row[...])
    col = jnp.where(gone, 0.0, raised_col[...])
    raised_row[...] = row
    raised_col[...] = col
    code = (place_col * HALF + mode_col + 1).astype(F32)
    sent = jnp.where(lane == mode_col, col[:, 0:1], col)
    sent = jnp.where(lane == 0, code, sent)
    spot_row = jnp.where(owner_row >= 0, rank_row * DEVICES + owner_row, -1)
    pick = (iota((REQS, SLOTS), 0) == spot_row).astype(F32).astype(BF16)
    row_high, row_low = split(row)
    col_high, col_low = split(sent)
    packed = dot(pick, jnp.concatenate([row_high, col_high, row_low, col_low], axis=1))
    packed = packed[:, : 2 * LANES] + packed[:, 2 * LANES :]
    for j in range(PLACES):
        part = packed[j * DEVICES : (j + 1) * DEVICES]
        outbox[pl.ds(j, DEVICES, stride=8), :] = part[:, :LANES]
        outbox[pl.ds(PLACES + j, DEVICES, stride=8), :] = part[:, LANES:]

    pl.semaphore_wait(barrier, DEVICES - 1)

    def tile(ref, d):
        return ref.at[pl.ds(pl.multiple_of(d * 8, 8), 8), :]

    def send(src, dst, which, peer):
        pltpu.make_async_remote_copy(
            src_ref=tile(src, peer),
            dst_ref=tile(dst, me),
            send_sem=send_sem.at[which],
            recv_sem=recv_sem.at[which],
            device_id=(peer // 32, lax.rem(peer, 32)),
            device_id_type=MESH,
        ).start()

    def keep(src, dst, which):
        return pltpu.make_async_copy(tile(src, me), tile(dst, me), local_sem.at[which])

    def wait_others(src, dst, sem):
        others = pl.ds(0, BOX - 8)
        pltpu.make_async_copy(src.at[others, :], dst.at[others, :], sem).wait()

    keep(outbox, inbox, 0).start()
    prepare_hamiltonian(hamiltonian, weights, left)
    get_folks.wait()

    def first_wait(i, carry):
        for n in range(8):
            peer = lax.rem(me + (i * 8 + n + 1) * STRIDE, DEVICES)
            if n < 7:
                send(outbox, inbox, 0, peer)
            else:
                @pl.when(i < 15)
                def _():
                    send(outbox, inbox, 0, peer)
        at = pl.ds(pl.multiple_of(i * CHUNK, CHUNK), CHUNK)
        x = folks[at, :]
        both = side_by_side(x)
        folks_t[at, :] = transposed_chunk(both)
        folks_done[at, :] = own_terms(x, both, i * 4, weights, left, damping_s, parent_modes_s, 3)
        x = kids[at, :]
        kids_part[at, :] = own_terms(x, side_by_side(x), i * 4, weights, left, damping_s, modes_s, 4)
        pltpu.make_async_copy(kids_part.at[at, :], kids_out.at[at, :], out_sem.at[0]).start()
        return carry

    lax.fori_loop(0, ROWS // CHUNK, first_wait, 0)

    def pick_near(a, carry):
        for s in range(4):
            line = jnp.minimum(source_s[s, a], HALF - 1) * HALF + modes_s[s, a]
            near_row[pl.ds(s * HALF + a, 1), :] = folks[pl.ds(line, 1), :]
            near_col[pl.ds(s * HALF + a, 1), :] = folks_t[pl.ds(line, 1), :]
        return carry

    lax.fori_loop(0, HALF, pick_near, 0, unroll=4)

    lines[:, REQS:] = jnp.where(q_row < HALF, q_row * HALF + mode_row, ROWS)
    for k in range(2):
        at = slice(k * LANES, (k + 1) * LANES)
        put_lines(raised_row[at, :], raised_col[at, :], rows, cols, REQS + k * LANES)

    keep(outbox, inbox, 0).wait()
    wait_others(outbox, inbox, recv_sem.at[0])

    codes = jnp.zeros((DEVICES, LANES), F32)
    across = iota((DEVICES, LANES), 1)
    for j in range(PLACES):
        codes = jnp.where(across == j, inbox[pl.ds(PLACES + j, DEVICES, stride=8), 0:1], codes)
    codes = jnp.clip(codes.T[:8, :].astype(I32) - 1, 0, 2 * HALF - 1)
    chosen = jnp.where(codes >= HALF, table[1:2, :], table[0:1, :])
    wanted = jnp.clip(chosen * HALF + lax.rem(codes, HALF), 0, ROWS - 1)
    targets[...] = wanted
    to_scalar = pltpu.make_async_copy(targets, targets_s, in_sem.at[2])
    to_scalar.start()

    to_scalar.wait()

    def answer(i, carry):
        for n in range(8):
            peer = lax.rem(me + (i * 8 + n + 1) * STRIDE, DEVICES)
            for j in range(PLACES):
                line = targets_s[j, peer]
                reply[pl.ds(peer * 8 + j, 1), :] = folks[pl.ds(line, 1), :]
                reply[pl.ds(peer * 8 + PLACES + j, 1), :] = folks_t[pl.ds(line, 1), :]
            if n < 7:
                send(reply, answers, 1, peer)
            else:
                @pl.when(i < 15)
                def _():
                    send(reply, answers, 1, peer)
        return carry

    lax.fori_loop(0, ROWS // CHUNK, answer, 0)
    keep(reply, answers, 1).start()

    for j in range(PLACES):
        row = inbox[pl.ds(j, DEVICES, stride=8), :]
        col = inbox[pl.ds(PLACES + j, DEVICES, stride=8), :]
        mode = lax.rem(jnp.maximum(col[:, 0:1].astype(I32) - 1, 0), HALF)
        hit = across == mode
        first = jnp.sum(jnp.where(hit, col, 0.0), axis=1, keepdims=True)
        first = jnp.where(mode == 0, 0.0, first)
        col = jnp.where(across == 0, first, jnp.where(hit, 0.0, col))
        put_lines(row, col, rows, cols, j * DEVICES)
        lines[:, j * DEVICES : (j + 1) * DEVICES] = wanted[j : j + 1, :]

    def add_raised(i, carry):
        base = pl.multiple_of(i * CHUNK, CHUNK)
        at = pl.ds(base, CHUNK)
        folks_done[at, :] = folks_done[at, :] + slot_sums(rows, cols, lines, base)
        pltpu.make_async_copy(folks_done.at[at, :], folks_out.at[at, :], out_sem.at[1]).start()
        return carry

    lax.fori_loop(0, ROWS // CHUNK, add_raised, 0, unroll=2)
    wait_others(outbox, inbox, send_sem.at[0])
    wait_others(reply, answers, send_sem.at[1])
    pltpu.make_async_copy(kids_part, kids_out, out_sem.at[0]).wait()
    pltpu.make_async_copy(folks_done, folks_out, out_sem.at[1]).wait()
    keep(reply, answers, 1).wait()
    wait_others(reply, answers, recv_sem.at[1])


def rates_kernel(
    live_s, modes, source, real, imag, answers, near_row, near_col, kids_part, folks_done,
    child_out, parent_out,
    part, done, through, rows, cols, lines, in_sem, out_sem,
):
    get_part = pltpu.make_async_copy(kids_part, part, in_sem.at[0])
    get_part.start()
    get_parents = pltpu.make_async_copy(folks_done, through, in_sem.at[1])
    get_parents.start()
    put_parents = pltpu.make_async_copy(through, parent_out, out_sem.at[0])

    q_row, mode_row = slots_row(source[...]), slots_row(modes[...])
    q_col, mode_col = as_column(q_row), as_column(mode_row)
    owner_col, rank_col, _, _ = slot_places(q_row, q_col)
    spot = jnp.where(owner_col >= 0, owner_col * 8 + rank_col, -8)
    spots = jnp.concatenate([spot, spot + PLACES], axis=0)
    pick = (iota((2 * SLOTS, BOX), 1) == spots).astype(F32).astype(BF16)
    got = dot(pick, side_by_side(answers[...]))
    got = got[:, :LANES] + got[:, LANES:]
    near = owner_col < 0
    row = jnp.where(near, near_row[...], got[:SLOTS])
    col = jnp.where(near, near_col[...], got[SLOTS:])
    lane = iota((SLOTS, LANES), 1)
    chosen = iota((SLOTS, HALF), 1) == mode_col
    factor = jnp.sum(jnp.where(chosen, real[...], 0.0), axis=1, keepdims=True)
    other = jnp.sum(jnp.where(chosen, imag[...], 0.0), axis=1, keepdims=True)
    signed = jnp.where(lane < HALF, -other, other)
    row = factor * row + signed * turn(row)
    col = factor * col - signed * turn(col)
    for k in range(2):
        at = slice(k * LANES, (k + 1) * LANES)
        put_lines(row[at], col[at], rows, cols, k * LANES)
    lines[...] = lax.rem(iota((1, SLOTS), 1), HALF) * HALF + mode_row
    limit = live_s[0] * HALF
    get_part.wait()
    get_parents.wait()
    put_parents.start()

    def add(i, carry):
        base = pl.multiple_of(i * CHUNK, CHUNK)
        at = pl.ds(base, CHUNK)
        result = part[at, :] + slot_sums(rows, cols, lines, base)
        alive = iota((CHUNK, LANES), 0) + base < limit
        done[at, :] = jnp.where(alive, result, 0.0)
        pltpu.make_async_copy(done.at[at, :], child_out.at[at, :], out_sem.at[1]).start()
        return carry

    lax.fori_loop(0, ROWS // CHUNK, add, 0, unroll=2)
    pltpu.make_async_copy(done, child_out, out_sem.at[1]).wait()
    put_parents.wait()


VMEM = pl.BlockSpec(memory_space=pltpu.VMEM)
SMEM = pl.BlockSpec(memory_space=pltpu.SMEM)
HBM = pl.BlockSpec(memory_space=pltpu.HBM)


def body(
    children, parents, hamiltonian, damping, coupling_real, coupling_imag,
    child_modes, child_source, parent_modes, send_rows, live_count,
):
    modes, source, parent_modes = child_modes.T, child_source.T, parent_modes.T
    lines = jax.ShapeDtypeStruct((SLOTS, LANES), F32)
    box = jax.ShapeDtypeStruct((BOX, LANES), F32)
    whole = jax.ShapeDtypeStruct((ROWS, LANES), F32)
    every = REQS + SLOTS
    answers, near_row, near_col, kids_part, folks_done = pl.pallas_call(
        exchange_kernel,
        out_shape=(box, lines, lines, whole, whole),
        in_specs=[SMEM] * 5 + [VMEM] * 4 + [HBM] * 2,
        out_specs=(HBM, VMEM, VMEM, HBM, HBM),
        scratch_shapes=[pltpu.VMEM((ROWS, LANES), F32)] * 6
        + [pltpu.VMEM((BOX, LANES), F32)] * 3
        + [pltpu.VMEM((SLOTS, LANES), F32)] * 2
        + [
            pltpu.VMEM((8, LANES), I32),
            pltpu.SMEM((8, LANES), I32),
            pltpu.VMEM((2 * LANES, 2 * LANES), BF16),
            pltpu.VMEM((HALF, 2 * LANES), BF16),
            pltpu.VMEM((every, 2 * LANES), BF16),
            pltpu.VMEM((2 * LANES, every), BF16),
            pltpu.VMEM((1, every), I32),
            pltpu.SemaphoreType.DMA((3,)),
            pltpu.SemaphoreType.DMA((2,)),
            pltpu.SemaphoreType.DMA((2,)),
            pltpu.SemaphoreType.DMA((2,)),
            pltpu.SemaphoreType.DMA((2,)),
        ],
        compiler_params=pltpu.CompilerParams(
            collective_id=0, has_side_effects=True, vmem_limit_bytes=60 * 2**20
        ),
    )(
        modes, source, parent_modes, live_count, damping, modes, source, send_rows[0].T, hamiltonian,
        children.reshape(ROWS, LANES), parents.reshape(ROWS, LANES),
    )
    child_rates, parent_rates = pl.pallas_call(
        rates_kernel,
        out_shape=(whole, whole),
        in_specs=[SMEM] + [VMEM] * 7 + [HBM] * 2,
        out_specs=(HBM, HBM),
        scratch_shapes=[
            pltpu.VMEM((ROWS, LANES), F32),
            pltpu.VMEM((ROWS, LANES), F32),
            pltpu.VMEM((ROWS, LANES), F32),
            pltpu.VMEM((SLOTS, 2 * LANES), BF16),
            pltpu.VMEM((2 * LANES, SLOTS), BF16),
            pltpu.VMEM((1, SLOTS), I32),
            pltpu.SemaphoreType.DMA((2,)),
            pltpu.SemaphoreType.DMA((2,)),
        ],
        compiler_params=pltpu.CompilerParams(vmem_limit_bytes=60 * 2**20),
    )(
        live_count, modes, source, coupling_real.reshape(1, HALF), coupling_imag.reshape(1, HALF),
        answers, near_row, near_col, kids_part, folks_done,
    )
    return child_rates.reshape(children.shape), parent_rates.reshape(parents.shape)


def solution(mesh):
    in_specs = (
        P(("lo", "hi"), None, None),
        P(("lo", "hi"), None, None),
        P(),
        P(),
        P(),
        P(),
        P(("lo", "hi"), None),
        P(("lo", "hi"), None),
        P(("lo", "hi"), None),
        P(("lo", "hi"), None, None),
        P(("lo", "hi")),
    )
    out_specs = (P(("lo", "hi"), None, None), P(("lo", "hi"), None, None))
    return jax.shard_map(body, mesh=mesh, in_specs=in_specs, out_specs=out_specs, check_vma=False)
```

```python
import jax
import jax.numpy as jnp
from jax import lax
from jax.experimental import pallas as pl
from jax.experimental.pallas import tpu as pltpu
from jax.sharding import PartitionSpec as P

LOGICAL = pl.DeviceIdType.LOGICAL
F32 = jnp.float32
BF16 = jnp.bfloat16
I32 = jnp.int32
LANES = 128
HALF = 64
ROWS = 4096
SLOTS = 256
PLACES = 4
CHUNK = 256
DEVICES = 128
STRIDE = 43
BOX = DEVICES * 2 * PLACES
REQS = DEVICES * PLACES


def iota(shape, axis):
    return lax.broadcasted_iota(I32, shape, axis)


def split(x):
    high = x.astype(BF16)
    return high, (x - high.astype(F32)).astype(BF16)


def side_by_side(x):
    return jnp.concatenate(split(x), axis=1)


def dot(a, b):
    return lax.dot_general(a, b, (((1,), (0,)), ((), ())), preferred_element_type=F32)


def dot_nt(a, b):
    return lax.dot_general(a, b, (((1,), (1,)), ((), ())), preferred_element_type=F32)


def turn(x):
    return pltpu.roll(x, HALF, 1)


def rearrange(flipped):
    left = iota((HALF, LANES), 1) < HALF
    blocks = []
    for pair in range(2):
        top = flipped[:HALF, pair * LANES : (pair + 1) * LANES]
        low = flipped[HALF:, pair * LANES : (pair + 1) * LANES]
        blocks.append(jnp.where(left, top, turn(low)))
        blocks.append(jnp.where(left, turn(top), low))
    return jnp.concatenate(blocks, axis=0)


def transposed_chunk(both):
    eye = (iota((LANES, 2 * LANES), 0) == lax.rem(iota((LANES, 2 * LANES), 1), LANES)).astype(F32).astype(BF16)
    return rearrange(dot_nt(eye, both))


def slots_row(table):
    twice = jnp.concatenate([table, table], axis=1)
    left = iota((1, LANES), 1) < HALF
    return jnp.concatenate([jnp.where(left, twice[s : s + 1], twice[s + 1 : s + 2]) for s in (0, 2)], axis=1)


def as_column(row):
    wide = jnp.broadcast_to(row.astype(F32), (LANES, row.shape[1]))
    parts = [wide[:, k : k + LANES].T for k in range(0, row.shape[1], LANES)]
    return jnp.concatenate(parts, axis=0)[:, 0:1].astype(I32)


def as_row(col):
    return jnp.broadcast_to(col.astype(F32), (col.shape[0], LANES)).T[0:1, :].astype(I32)


def slot_places(q_row, q_col):
    owner_col = jnp.where(q_col >= HALF, (q_col - HALF) >> 1, -1)
    owner_row = jnp.where(q_row >= HALF, (q_row - HALF) >> 1, -1)
    same = (owner_col == owner_row).astype(I32)
    down, across = iota((SLOTS, SLOTS), 0), iota((SLOTS, SLOTS), 1)
    before = jnp.where(across < down, same, 0).astype(F32)
    after = jnp.where(down < across, same, 0).astype(F32)
    rank_col = jnp.sum(before, axis=1, keepdims=True).astype(I32)
    rank_row = jnp.sum(after, axis=0, keepdims=True).astype(I32)
    return owner_col, rank_col, owner_row, rank_row


def times_minus_i(x):
    y = turn(x)
    return jnp.where(iota(x.shape, 1) < HALF, y, -y)


def prepare_hamiltonian(hamiltonian, weights, left):
    h = hamiltonian[...]
    wide = jnp.concatenate([h, h], axis=1)
    tall = jnp.concatenate([wide] * 4, axis=0)
    down, across = iota((2 * LANES, LANES), 0), iota((2 * LANES, LANES), 1)
    lower = lax.rem(down // HALF, 2) == 1
    square = jnp.where(lower == (across < HALF), jnp.where(lower, tall, -tall), 0.0)
    weights[...] = side_by_side(square)
    high, low = split(wide)
    left[...] = jnp.concatenate([high, low], axis=1)


def own_terms(x, both, first, weights, left, damping_s, modes_s, places):
    right = dot(both, weights[...])
    right = right[:, :LANES] + right[:, LANES:]
    lefts = []
    for pair in range(2):
        a, b = (both[(2 * pair + n) * HALF : (2 * pair + n + 1) * HALF] for n in range(2))
        a = jnp.concatenate([a[:, :LANES], a[:, LANES:]], axis=0)
        b = jnp.concatenate([b[:, :LANES], b[:, LANES:]], axis=0)
        ab = jnp.concatenate([a, b], axis=1)
        product = dot(left[...], jnp.concatenate([ab, ab], axis=0))
        lefts += [product[:, :LANES], product[:, LANES:]]
    part = times_minus_i(jnp.concatenate(lefts, axis=0)) - right
    results = []
    for k in range(4):
        rate = damping_s[modes_s[0, first + k]]
        for s in range(1, places):
            rate = rate + damping_s[modes_s[s, first + k]]
        at = slice(k * HALF, (k + 1) * HALF)
        results.append(part[at] - rate * x[at])
    return jnp.concatenate(results, axis=0)


def slot_sums(rows, cols, line, base):
    hot = (iota((CHUNK, line.shape[1]), 0) + base == line[...]).astype(F32).astype(BF16)
    more = dot(hot, rows[...])
    less = dot_nt(cols[...], hot)
    return more[:, :LANES] + more[:, LANES:] + rearrange(less[:LANES] + less[LANES:])


def put_lines(row, col, rows, cols, at):
    rows[at : at + LANES, :] = side_by_side(times_minus_i(row))
    cols[:, at : at + LANES] = jnp.concatenate(split(-times_minus_i(col).T), axis=0)


def exchange_kernel(
    modes_s, source_s, parent_modes_s, live_s, damping_s, modes, source, table, hamiltonian, children, parents,
    answers, near_row, near_col, kids_out, folks_out,
    kids, kids_t, folks, folks_t, kids_part, folks_done, outbox, inbox, reply, raised_row, raised_col, targets, targets_s,
    weights, left, rows, cols, lines,
    in_sem, out_sem, local_sem, send_sem, recv_sem,
):
    lo, hi = lax.axis_index("lo"), lax.axis_index("hi")
    me = lo * 32 + hi
    get_kids = pltpu.make_async_copy(children, kids, in_sem.at[0])
    get_folks = pltpu.make_async_copy(parents, folks, in_sem.at[1])
    get_kids.start()

    barrier = pltpu.get_barrier_semaphore()

    def greet(k, carry):
        peer = lax.rem(me + k, DEVICES)
        pl.semaphore_signal(barrier, 1, device_id=peer, device_id_type=LOGICAL)
        return carry

    lax.fori_loop(1, DEVICES, greet, 0)

    q_row, mode_row = slots_row(source[...]), slots_row(modes[...])
    q_col, mode_col = as_column(q_row), as_column(mode_row)
    _, _, owner_row, rank_row = slot_places(q_row, q_col)
    place_col = lax.rem(jnp.maximum(q_col - HALF, 0), 2)
    alive_col = lax.rem(iota((SLOTS, 1), 0), HALF) < live_s[0]

    get_kids.wait()
    get_folks.start()

    def turn_kids(i, carry):
        at = pl.ds(pl.multiple_of(i * CHUNK, CHUNK), CHUNK)
        kids_t[at, :] = transposed_chunk(side_by_side(kids[at, :]))
        return carry

    lax.fori_loop(0, ROWS // CHUNK, turn_kids, 0, unroll=4)

    def pick_kids(a, carry):
        for s in range(4):
            line = a * HALF + modes_s[s, a]
            raised_row[pl.ds(s * HALF + a, 1), :] = kids[pl.ds(line, 1), :]
            raised_col[pl.ds(s * HALF + a, 1), :] = kids_t[pl.ds(line, 1), :]
        return carry

    lax.fori_loop(0, HALF, pick_kids, 0, unroll=4)

    lane = iota((SLOTS, LANES), 1)
    diagonal = lax.rem(lane, HALF) == mode_col
    gone = diagonal | jnp.logical_not(alive_col)
    row = jnp.where(gone, 0.0, raised_row[...])
    col = jnp.where(gone, 0.0, raised_col[...])
    raised_row[...] = row
    raised_col[...] = col
    code = (place_col * HALF + mode_col + 1).astype(F32)
    sent = jnp.where(lane == mode_col, col[:, 0:1], col)
    sent = jnp.where(lane == 0, code, sent)
    spot_row = jnp.where(owner_row >= 0, rank_row * DEVICES + owner_row, -1)
    pick = (iota((REQS, SLOTS), 0) == spot_row).astype(F32).astype(BF16)
    row_high, row_low = split(row)
    col_high, col_low = split(sent)
    packed = dot(pick, jnp.concatenate([row_high, col_high, row_low, col_low], axis=1))
    packed = packed[:, : 2 * LANES] + packed[:, 2 * LANES :]
    for j in range(PLACES):
        part = packed[j * DEVICES : (j + 1) * DEVICES]
        outbox[pl.ds(j, DEVICES, stride=8), :] = part[:, :LANES]
        outbox[pl.ds(PLACES + j, DEVICES, stride=8), :] = part[:, LANES:]

    pl.semaphore_wait(barrier, DEVICES - 1)

    def tile(ref, d):
        return ref.at[pl.ds(pl.multiple_of(d * 8, 8), 8), :]

    def send(src, dst, which, peer):
        pltpu.make_async_remote_copy(
            src_ref=tile(src, peer),
            dst_ref=tile(dst, me),
            send_sem=send_sem.at[which],
            recv_sem=recv_sem.at[which],
            device_id=peer,
            device_id_type=LOGICAL,
        ).start()

    def chunks(work):
        def body(i, carry):
            work(i, 8)
            return carry

        last = ROWS // CHUNK - 1
        lax.fori_loop(0, last, body, 0, unroll=3)
        work(last, 7)

    def keep(src, dst, which):
        return pltpu.make_async_copy(tile(src, me), tile(dst, me), local_sem.at[which])

    def wait_others(src, dst, sem):
        others = pl.ds(0, BOX - 8)
        pltpu.make_async_copy(src.at[others, :], dst.at[others, :], sem).wait()

    keep(outbox, inbox, 0).start()
    prepare_hamiltonian(hamiltonian, weights, left)
    get_folks.wait()

    def first_wait(i, count):
        for n in range(count):
            send(outbox, inbox, 0, lax.rem(me + (i * 8 + n + 1) * STRIDE, DEVICES))
        at = pl.ds(pl.multiple_of(i * CHUNK, CHUNK), CHUNK)
        x = folks[at, :]
        both = side_by_side(x)
        folks_t[at, :] = transposed_chunk(both)
        folks_done[at, :] = own_terms(x, both, i * 4, weights, left, damping_s, parent_modes_s, 3)
        x = kids[at, :]
        kids_part[at, :] = own_terms(x, side_by_side(x), i * 4, weights, left, damping_s, modes_s, 4)
        pltpu.make_async_copy(kids_part.at[at, :], kids_out.at[at, :], out_sem.at[0]).start()

    chunks(first_wait)

    def pick_near(a, carry):
        for s in range(4):
            line = jnp.minimum(source_s[s, a], HALF - 1) * HALF + modes_s[s, a]
            near_row[pl.ds(s * HALF + a, 1), :] = folks[pl.ds(line, 1), :]
            near_col[pl.ds(s * HALF + a, 1), :] = folks_t[pl.ds(line, 1), :]
        return carry

    lax.fori_loop(0, HALF, pick_near, 0, unroll=4)

    lines[:, REQS:] = jnp.where(q_row < HALF, q_row * HALF + mode_row, ROWS)
    for k in range(2):
        at = slice(k * LANES, (k + 1) * LANES)
        put_lines(raised_row[at, :], raised_col[at, :], rows, cols, REQS + k * LANES)

    keep(outbox, inbox, 0).wait()
    wait_others(outbox, inbox, recv_sem.at[0])

    codes = jnp.zeros((DEVICES, LANES), F32)
    across = iota((DEVICES, LANES), 1)
    for j in range(PLACES):
        codes = jnp.where(across == j, inbox[pl.ds(PLACES + j, DEVICES, stride=8), 0:1], codes)
    codes = jnp.clip(codes.T[:8, :].astype(I32) - 1, 0, 2 * HALF - 1)
    chosen = jnp.where(codes >= HALF, table[1:2, :], table[0:1, :])
    wanted = jnp.clip(chosen * HALF + lax.rem(codes, HALF), 0, ROWS - 1)
    targets[...] = wanted
    to_scalar = pltpu.make_async_copy(targets, targets_s, in_sem.at[2])
    to_scalar.start()

    to_scalar.wait()

    def answer(i, count):
        peers = [lax.rem(me + (i * 8 + n + 1) * STRIDE, DEVICES) for n in range(8)]
        for peer in peers:
            for j in range(PLACES):
                line = targets_s[j, peer]
                reply[pl.ds(peer * 8 + j, 1), :] = folks[pl.ds(line, 1), :]
                reply[pl.ds(peer * 8 + PLACES + j, 1), :] = folks_t[pl.ds(line, 1), :]
        for peer in peers[:count]:
            send(reply, answers, 1, peer)

    chunks(answer)
    keep(reply, answers, 1).start()

    for j in range(PLACES):
        row = inbox[pl.ds(j, DEVICES, stride=8), :]
        col = inbox[pl.ds(PLACES + j, DEVICES, stride=8), :]
        mode = lax.rem(jnp.maximum(col[:, 0:1].astype(I32) - 1, 0), HALF)
        hit = across == mode
        first = jnp.sum(jnp.where(hit, col, 0.0), axis=1, keepdims=True)
        first = jnp.where(mode == 0, 0.0, first)
        col = jnp.where(across == 0, first, jnp.where(hit, 0.0, col))
        put_lines(row, col, rows, cols, j * DEVICES)
        lines[:, j * DEVICES : (j + 1) * DEVICES] = wanted[j : j + 1, :]

    def add_raised(i, carry):
        base = pl.multiple_of(i * CHUNK, CHUNK)
        at = pl.ds(base, CHUNK)
        folks_done[at, :] = folks_done[at, :] + slot_sums(rows, cols, lines, base)
        pltpu.make_async_copy(folks_done.at[at, :], folks_out.at[at, :], out_sem.at[1]).start()
        return carry

    lax.fori_loop(0, ROWS // CHUNK, add_raised, 0, unroll=4)
    wait_others(outbox, inbox, send_sem.at[0])
    wait_others(reply, answers, send_sem.at[1])
    pltpu.make_async_copy(kids_part, kids_out, out_sem.at[0]).wait()
    pltpu.make_async_copy(folks_done, folks_out, out_sem.at[1]).wait()
    keep(reply, answers, 1).wait()
    wait_others(reply, answers, recv_sem.at[1])


def rates_kernel(
    live_s, modes, source, real, imag, answers, near_row, near_col, kids_part, folks_done,
    child_out, parent_out,
    part, done, through, rows, cols, lines, in_sem, out_sem,
):
    get_part = pltpu.make_async_copy(kids_part, part, in_sem.at[0])
    get_part.start()
    get_parents = pltpu.make_async_copy(folks_done, through, in_sem.at[1])
    get_parents.start()
    put_parents = pltpu.make_async_copy(through, parent_out, out_sem.at[0])

    q_row, mode_row = slots_row(source[...]), slots_row(modes[...])
    q_col, mode_col = as_column(q_row), as_column(mode_row)
    owner_col, rank_col, _, _ = slot_places(q_row, q_col)
    spot = jnp.where(owner_col >= 0, owner_col * 8 + rank_col, -8)
    spots = jnp.concatenate([spot, spot + PLACES], axis=0)
    pick = (iota((2 * SLOTS, BOX), 1) == spots).astype(F32).astype(BF16)
    got = dot(pick, side_by_side(answers[...]))
    got = got[:, :LANES] + got[:, LANES:]
    near = owner_col < 0
    row = jnp.where(near, near_row[...], got[:SLOTS])
    col = jnp.where(near, near_col[...], got[SLOTS:])
    lane = iota((SLOTS, LANES), 1)
    chosen = iota((SLOTS, HALF), 1) == mode_col
    factor = jnp.sum(jnp.where(chosen, real[...], 0.0), axis=1, keepdims=True)
    other = jnp.sum(jnp.where(chosen, imag[...], 0.0), axis=1, keepdims=True)
    signed = jnp.where(lane < HALF, -other, other)
    row = factor * row + signed * turn(row)
    col = factor * col - signed * turn(col)
    for k in range(2):
        at = slice(k * LANES, (k + 1) * LANES)
        put_lines(row[at], col[at], rows, cols, k * LANES)
    lines[...] = lax.rem(iota((1, SLOTS), 1), HALF) * HALF + mode_row
    limit = live_s[0] * HALF
    get_part.wait()
    get_parents.wait()
    put_parents.start()

    def add(i, carry):
        base = pl.multiple_of(i * CHUNK, CHUNK)
        at = pl.ds(base, CHUNK)
        result = part[at, :] + slot_sums(rows, cols, lines, base)
        alive = iota((CHUNK, LANES), 0) + base < limit
        done[at, :] = jnp.where(alive, result, 0.0)
        pltpu.make_async_copy(done.at[at, :], child_out.at[at, :], out_sem.at[1]).start()
        return carry

    lax.fori_loop(0, ROWS // CHUNK, add, 0, unroll=4)
    pltpu.make_async_copy(done, child_out, out_sem.at[1]).wait()
    put_parents.wait()


VMEM = pl.BlockSpec(memory_space=pltpu.VMEM)
SMEM = pl.BlockSpec(memory_space=pltpu.SMEM)
HBM = pl.BlockSpec(memory_space=pltpu.HBM)


def body(
    children, parents, hamiltonian, damping, coupling_real, coupling_imag,
    child_modes, child_source, parent_modes, send_rows, live_count,
):
    modes, source, parent_modes = child_modes.T, child_source.T, parent_modes.T
    lines = jax.ShapeDtypeStruct((SLOTS, LANES), F32)
    box = jax.ShapeDtypeStruct((BOX, LANES), F32)
    whole = jax.ShapeDtypeStruct((ROWS, LANES), F32)
    every = REQS + SLOTS
    answers, near_row, near_col, kids_part, folks_done = pl.pallas_call(
        exchange_kernel,
        out_shape=(box, lines, lines, whole, whole),
        in_specs=[SMEM] * 5 + [VMEM] * 4 + [HBM] * 2,
        out_specs=(HBM, VMEM, VMEM, HBM, HBM),
        scratch_shapes=[pltpu.VMEM((ROWS, LANES), F32)] * 6
        + [pltpu.VMEM((BOX, LANES), F32)] * 3
        + [pltpu.VMEM((SLOTS, LANES), F32)] * 2
        + [
            pltpu.VMEM((8, LANES), I32),
            pltpu.SMEM((8, LANES), I32),
            pltpu.VMEM((2 * LANES, 2 * LANES), BF16),
            pltpu.VMEM((HALF, 2 * LANES), BF16),
            pltpu.VMEM((every, 2 * LANES), BF16),
            pltpu.VMEM((2 * LANES, every), BF16),
            pltpu.VMEM((1, every), I32),
            pltpu.SemaphoreType.DMA((3,)),
            pltpu.SemaphoreType.DMA((2,)),
            pltpu.SemaphoreType.DMA((2,)),
            pltpu.SemaphoreType.DMA((2,)),
            pltpu.SemaphoreType.DMA((2,)),
        ],
        compiler_params=pltpu.CompilerParams(
            collective_id=0, has_side_effects=True, vmem_limit_bytes=60 * 2**20
        ),
    )(
        modes, source, parent_modes, live_count, damping, modes, source, send_rows[0].T, hamiltonian,
        children.reshape(ROWS, LANES), parents.reshape(ROWS, LANES),
    )
    child_rates, parent_rates = pl.pallas_call(
        rates_kernel,
        out_shape=(whole, whole),
        in_specs=[SMEM] + [VMEM] * 7 + [HBM] * 2,
        out_specs=(HBM, HBM),
        scratch_shapes=[
            pltpu.VMEM((ROWS, LANES), F32),
            pltpu.VMEM((ROWS, LANES), F32),
            pltpu.VMEM((ROWS, LANES), F32),
            pltpu.VMEM((SLOTS, 2 * LANES), BF16),
            pltpu.VMEM((2 * LANES, SLOTS), BF16),
            pltpu.VMEM((1, SLOTS), I32),
            pltpu.SemaphoreType.DMA((2,)),
            pltpu.SemaphoreType.DMA((2,)),
        ],
        compiler_params=pltpu.CompilerParams(vmem_limit_bytes=60 * 2**20),
    )(
        live_count, modes, source, coupling_real.reshape(1, HALF), coupling_imag.reshape(1, HALF),
        answers, near_row, near_col, kids_part, folks_done,
    )
    return child_rates.reshape(children.shape), parent_rates.reshape(parents.shape)


def solution(mesh):
    in_specs = (
        P(("lo", "hi"), None, None),
        P(("lo", "hi"), None, None),
        P(),
        P(),
        P(),
        P(),
        P(("lo", "hi"), None),
        P(("lo", "hi"), None),
        P(("lo", "hi"), None),
        P(("lo", "hi"), None, None),
        P(("lo", "hi")),
    )
    out_specs = (P(("lo", "hi"), None, None), P(("lo", "hi"), None, None))
    return jax.shard_map(body, mesh=mesh, in_specs=in_specs, out_specs=out_specs, check_vma=False)
```

```python
import jax
import jax.numpy as jnp
from jax import lax
from jax.experimental import pallas as pl
from jax.experimental.pallas import tpu as pltpu
from jax.sharding import PartitionSpec as P

LOGICAL = pl.DeviceIdType.LOGICAL
F32 = jnp.float32
BF16 = jnp.bfloat16
I32 = jnp.int32
LANES = 128
HALF = 64
ROWS = 4096
SLOTS = 256
PLACES = 4
CHUNK = 256
DEVICES = 128
STRIDE = 43
BOX = DEVICES * 2 * PLACES
REQS = DEVICES * PLACES


def iota(shape, axis):
    return lax.broadcasted_iota(I32, shape, axis)


def split(x):
    high = x.astype(BF16)
    return high, (x - high.astype(F32)).astype(BF16)


def side_by_side(x):
    return jnp.concatenate(split(x), axis=1)


def dot(a, b):
    return lax.dot_general(a, b, (((1,), (0,)), ((), ())), preferred_element_type=F32)


def dot_nt(a, b):
    return lax.dot_general(a, b, (((1,), (1,)), ((), ())), preferred_element_type=F32)


def turn(x):
    return pltpu.roll(x, HALF, 1)


def rearrange(flipped):
    left = iota((HALF, LANES), 1) < HALF
    blocks = []
    for pair in range(2):
        top = flipped[:HALF, pair * LANES : (pair + 1) * LANES]
        low = flipped[HALF:, pair * LANES : (pair + 1) * LANES]
        blocks.append(jnp.where(left, top, turn(low)))
        blocks.append(jnp.where(left, turn(top), low))
    return jnp.concatenate(blocks, axis=0)


def transposed_chunk(both):
    eye = (iota((LANES, 2 * LANES), 0) == lax.rem(iota((LANES, 2 * LANES), 1), LANES)).astype(F32).astype(BF16)
    return rearrange(dot_nt(eye, both))


def slots_row(table):
    twice = jnp.concatenate([table, table], axis=1)
    left = iota((1, LANES), 1) < HALF
    return jnp.concatenate([jnp.where(left, twice[s : s + 1], twice[s + 1 : s + 2]) for s in (0, 2)], axis=1)


def as_column(row):
    wide = jnp.broadcast_to(row.astype(F32), (LANES, row.shape[1]))
    parts = [wide[:, k : k + LANES].T for k in range(0, row.shape[1], LANES)]
    return jnp.concatenate(parts, axis=0)[:, 0:1].astype(I32)


def as_row(col):
    return jnp.broadcast_to(col.astype(F32), (col.shape[0], LANES)).T[0:1, :].astype(I32)


def slot_places(q_row, q_col):
    owner_col = jnp.where(q_col >= HALF, (q_col - HALF) >> 1, -1)
    owner_row = jnp.where(q_row >= HALF, (q_row - HALF) >> 1, -1)
    same = (owner_col == owner_row).astype(I32)
    down, across = iota((SLOTS, SLOTS), 0), iota((SLOTS, SLOTS), 1)
    before = jnp.where(across < down, same, 0).astype(F32)
    after = jnp.where(down < across, same, 0).astype(F32)
    rank_col = jnp.sum(before, axis=1, keepdims=True).astype(I32)
    rank_row = jnp.sum(after, axis=0, keepdims=True).astype(I32)
    return owner_col, rank_col, owner_row, rank_row


def times_minus_i(x):
    y = turn(x)
    return jnp.where(iota(x.shape, 1) < HALF, y, -y)


def prepare_hamiltonian(hamiltonian, weights, left):
    h = hamiltonian[...]
    wide = jnp.concatenate([h, h], axis=1)
    tall = jnp.concatenate([wide] * 4, axis=0)
    down, across = iota((2 * LANES, LANES), 0), iota((2 * LANES, LANES), 1)
    lower = lax.rem(down // HALF, 2) == 1
    square = jnp.where(lower == (across < HALF), jnp.where(lower, tall, -tall), 0.0)
    weights[...] = side_by_side(square)
    high, low = split(wide)
    left[...] = jnp.concatenate([high, low], axis=1)


def own_terms(x, both, first, weights, left, damping_s, modes_s, places):
    right = dot(both, weights[...])
    right = right[:, :LANES] + right[:, LANES:]
    lefts = []
    for pair in range(2):
        a, b = (both[(2 * pair + n) * HALF : (2 * pair + n + 1) * HALF] for n in range(2))
        a = jnp.concatenate([a[:, :LANES], a[:, LANES:]], axis=0)
        b = jnp.concatenate([b[:, :LANES], b[:, LANES:]], axis=0)
        ab = jnp.concatenate([a, b], axis=1)
        product = dot(left[...], jnp.concatenate([ab, ab], axis=0))
        lefts += [product[:, :LANES], product[:, LANES:]]
    part = times_minus_i(jnp.concatenate(lefts, axis=0)) - right
    results = []
    for k in range(4):
        rate = damping_s[modes_s[0, first + k]]
        for s in range(1, places):
            rate = rate + damping_s[modes_s[s, first + k]]
        at = slice(k * HALF, (k + 1) * HALF)
        results.append(part[at] - rate * x[at])
    return jnp.concatenate(results, axis=0)


def slot_sums(rows, cols, line, base):
    hot = (iota((CHUNK, line.shape[1]), 0) + base == line[...]).astype(F32).astype(BF16)
    more = dot(hot, rows[...])
    less = dot_nt(cols[...], hot)
    return more[:, :LANES] + more[:, LANES:] + rearrange(less[:LANES] + less[LANES:])


def put_lines(row, col, rows, cols, at):
    rows[at : at + LANES, :] = side_by_side(times_minus_i(row))
    cols[:, at : at + LANES] = jnp.concatenate(split(-times_minus_i(col).T), axis=0)


def exchange_kernel(
    modes_s, source_s, parent_modes_s, live_s, damping_s, modes_h, source_h, table_h, hamiltonian_h, children, parents,
    answers, near_row_out, near_col_out, kids_out, folks_out,
    kids, kids_t, folks, folks_t, kids_part, folks_done, outbox, inbox, reply,
    raised_row, raised_col, near_row, near_col, modes, source, table, hamiltonian, targets, targets_s,
    weights, left, rows, cols, lines,
    in_sem, small_sem, kids_sem, out_sem, local_sem, send_sem, recv_sem,
):
    lo, hi = lax.axis_index("lo"), lax.axis_index("hi")
    me = lo * 32 + hi
    quarter = ROWS // 4
    get_kids = []
    for k in range(4):
        at = pl.ds(k * quarter, quarter)
        get_kids.append(pltpu.make_async_copy(children.at[at, :], kids.at[at, :], kids_sem.at[k]))
    get_small = [
        pltpu.make_async_copy(src, dst, small_sem.at[k])
        for k, (src, dst) in enumerate(
            ((modes_h, modes), (source_h, source), (table_h, table), (hamiltonian_h, hamiltonian))
        )
    ]
    get_folks = pltpu.make_async_copy(parents, folks, in_sem.at[1])
    for copy in get_small[:2] + get_kids + get_small[2:]:
        copy.start()

    barrier = pltpu.get_barrier_semaphore()

    def greet(k, carry):
        peer = lax.rem(me + k, DEVICES)
        pl.semaphore_signal(barrier, 1, device_id=peer, device_id_type=LOGICAL)
        return carry

    lax.fori_loop(1, DEVICES, greet, 0)
    get_folks.start()
    for copy in get_small[:2]:
        copy.wait()

    q_row, mode_row = slots_row(source[...]), slots_row(modes[...])
    q_col, mode_col = as_column(q_row), as_column(mode_row)
    _, _, owner_row, rank_row = slot_places(q_row, q_col)
    place_col = lax.rem(jnp.maximum(q_col - HALF, 0), 2)
    alive_col = lax.rem(iota((SLOTS, 1), 0), HALF) < live_s[0]


    def turn_kids(i, carry):
        at = pl.ds(pl.multiple_of(i * CHUNK, CHUNK), CHUNK)
        kids_t[at, :] = transposed_chunk(side_by_side(kids[at, :]))
        return carry

    for k in range(4):
        get_kids[k].wait()
        lax.fori_loop(4 * k, 4 * k + 4, turn_kids, 0, unroll=4)

    def pick_kids(a, carry):
        for s in range(4):
            line = a * HALF + modes_s[s, a]
            raised_row[pl.ds(s * HALF + a, 1), :] = kids[pl.ds(line, 1), :]
            raised_col[pl.ds(s * HALF + a, 1), :] = kids_t[pl.ds(line, 1), :]
        return carry

    lax.fori_loop(0, HALF, pick_kids, 0, unroll=4)

    lane = iota((SLOTS, LANES), 1)
    diagonal = lax.rem(lane, HALF) == mode_col
    gone = diagonal | jnp.logical_not(alive_col)
    row = jnp.where(gone, 0.0, raised_row[...])
    col = jnp.where(gone, 0.0, raised_col[...])
    raised_row[...] = row
    raised_col[...] = col
    code = (place_col * HALF + mode_col + 1).astype(F32)
    sent = jnp.where(lane == mode_col, col[:, 0:1], col)
    sent = jnp.where(lane == 0, code, sent)
    spot_row = jnp.where(owner_row >= 0, rank_row * DEVICES + owner_row, -1)
    pick = (iota((REQS, SLOTS), 0) == spot_row).astype(F32).astype(BF16)
    row_high, row_low = split(row)
    col_high, col_low = split(sent)
    packed = dot(pick, jnp.concatenate([row_high, col_high, row_low, col_low], axis=1))
    packed = packed[:, : 2 * LANES] + packed[:, 2 * LANES :]
    for j in range(PLACES):
        part = packed[j * DEVICES : (j + 1) * DEVICES]
        outbox[pl.ds(j, DEVICES, stride=8), :] = part[:, :LANES]
        outbox[pl.ds(PLACES + j, DEVICES, stride=8), :] = part[:, LANES:]

    pl.semaphore_wait(barrier, DEVICES - 1)

    def tile(ref, d):
        return ref.at[pl.ds(pl.multiple_of(d * 8, 8), 8), :]

    def send(src, dst, which, peer):
        pltpu.make_async_remote_copy(
            src_ref=tile(src, peer),
            dst_ref=tile(dst, me),
            send_sem=send_sem.at[which],
            recv_sem=recv_sem.at[which],
            device_id=peer,
            device_id_type=LOGICAL,
        ).start()

    def chunks(work):
        def body(i, carry):
            work(i, 8)
            return carry

        last = ROWS // CHUNK - 1
        lax.fori_loop(0, last, body, 0, unroll=3)
        work(last, 7)

    def keep(src, dst, which):
        return pltpu.make_async_copy(tile(src, me), tile(dst, me), local_sem.at[which])

    def wait_others(src, dst, sem):
        others = pl.ds(0, BOX - 8)
        pltpu.make_async_copy(src.at[others, :], dst.at[others, :], sem).wait()

    keep(outbox, inbox, 0).start()
    def give(k, carry):
        send(outbox, inbox, 0, lax.rem(me + k * STRIDE, DEVICES))
        return carry

    lax.fori_loop(1, DEVICES, give, 0)

    for copy in get_small[2:]:
        copy.wait()
    prepare_hamiltonian(hamiltonian, weights, left)
    get_folks.wait()

    def first_wait(i, carry):
        at = pl.ds(pl.multiple_of(i * CHUNK, CHUNK), CHUNK)
        x = folks[at, :]
        both = side_by_side(x)
        folks_t[at, :] = transposed_chunk(both)
        folks_done[at, :] = own_terms(x, both, i * 4, weights, left, damping_s, parent_modes_s, 3)
        x = kids[at, :]
        kids_part[at, :] = own_terms(x, side_by_side(x), i * 4, weights, left, damping_s, modes_s, 4)
        pltpu.make_async_copy(kids_part.at[at, :], kids_out.at[at, :], out_sem.at[0]).start()
        return carry

    lax.fori_loop(0, ROWS // CHUNK, first_wait, 0, unroll=4)

    def pick_near(a, carry):
        for s in range(4):
            line = jnp.minimum(source_s[s, a], HALF - 1) * HALF + modes_s[s, a]
            near_row[pl.ds(s * HALF + a, 1), :] = folks[pl.ds(line, 1), :]
            near_col[pl.ds(s * HALF + a, 1), :] = folks_t[pl.ds(line, 1), :]
        return carry

    lax.fori_loop(0, HALF, pick_near, 0, unroll=4)
    put_near = [
        pltpu.make_async_copy(near_row, near_row_out, out_sem.at[2]),
        pltpu.make_async_copy(near_col, near_col_out, out_sem.at[3]),
    ]
    for copy in put_near:
        copy.start()

    lines[:, REQS:] = jnp.where(q_row < HALF, q_row * HALF + mode_row, ROWS)
    for k in range(2):
        at = slice(k * LANES, (k + 1) * LANES)
        put_lines(raised_row[at, :], raised_col[at, :], rows, cols, REQS + k * LANES)

    keep(outbox, inbox, 0).wait()
    wait_others(outbox, inbox, recv_sem.at[0])

    codes = jnp.zeros((DEVICES, LANES), F32)
    across = iota((DEVICES, LANES), 1)
    for j in range(PLACES):
        codes = jnp.where(across == j, inbox[pl.ds(PLACES + j, DEVICES, stride=8), 0:1], codes)
    codes = jnp.clip(codes.T[:8, :].astype(I32) - 1, 0, 2 * HALF - 1)
    chosen = jnp.where(codes >= HALF, table[1:2, :], table[0:1, :])
    wanted = jnp.clip(chosen * HALF + lax.rem(codes, HALF), 0, ROWS - 1)
    targets[...] = wanted
    to_scalar = pltpu.make_async_copy(targets, targets_s, in_sem.at[2])
    to_scalar.start()

    to_scalar.wait()

    def answer(i, count):
        peers = [lax.rem(me + (i * 8 + n + 1) * STRIDE, DEVICES) for n in range(8)]
        for peer in peers:
            for j in range(PLACES):
                line = targets_s[j, peer]
                reply[pl.ds(peer * 8 + j, 1), :] = folks[pl.ds(line, 1), :]
                reply[pl.ds(peer * 8 + PLACES + j, 1), :] = folks_t[pl.ds(line, 1), :]
        for peer in peers[:count]:
            send(reply, answers, 1, peer)

    chunks(answer)
    keep(reply, answers, 1).start()

    for j in range(PLACES):
        row = inbox[pl.ds(j, DEVICES, stride=8), :]
        col = inbox[pl.ds(PLACES + j, DEVICES, stride=8), :]
        mode = lax.rem(jnp.maximum(col[:, 0:1].astype(I32) - 1, 0), HALF)
        hit = across == mode
        first = jnp.sum(jnp.where(hit, col, 0.0), axis=1, keepdims=True)
        first = jnp.where(mode == 0, 0.0, first)
        col = jnp.where(across == 0, first, jnp.where(hit, 0.0, col))
        put_lines(row, col, rows, cols, j * DEVICES)
        lines[:, j * DEVICES : (j + 1) * DEVICES] = wanted[j : j + 1, :]

    def add_raised(i, carry):
        base = pl.multiple_of(i * CHUNK, CHUNK)
        at = pl.ds(base, CHUNK)
        folks_done[at, :] = folks_done[at, :] + slot_sums(rows, cols, lines, base)
        pltpu.make_async_copy(folks_done.at[at, :], folks_out.at[at, :], out_sem.at[1]).start()
        return carry

    lax.fori_loop(0, ROWS // CHUNK, add_raised, 0, unroll=4)
    wait_others(outbox, inbox, send_sem.at[0])
    wait_others(reply, answers, send_sem.at[1])
    for copy in put_near:
        copy.wait()
    pltpu.make_async_copy(kids_part, kids_out, out_sem.at[0]).wait()
    pltpu.make_async_copy(folks_done, folks_out, out_sem.at[1]).wait()
    keep(reply, answers, 1).wait()
    wait_others(reply, answers, recv_sem.at[1])


def rates_kernel(
    live_s, modes_h, source_h, real_h, imag_h, answers_h, near_row_h, near_col_h, kids_part, folks_done,
    child_out, parent_out,
    part, done, through, answers, near_row, near_col, modes, source, real, imag, rows, cols, lines,
    in_sem, small_sem, out_sem,
):
    get_small = [
        pltpu.make_async_copy(src, dst, small_sem.at[k])
        for k, (src, dst) in enumerate(
            (
                (modes_h, modes), (source_h, source), (answers_h, answers), (near_row_h, near_row),
                (near_col_h, near_col), (real_h, real), (imag_h, imag),
            )
        )
    ]
    for copy in get_small:
        copy.start()
    get_part = pltpu.make_async_copy(kids_part, part, in_sem.at[0])
    get_part.start()
    get_parents = pltpu.make_async_copy(folks_done, through, in_sem.at[1])
    get_parents.start()
    put_parents = pltpu.make_async_copy(through, parent_out, out_sem.at[0])
    for copy in get_small[:2]:
        copy.wait()

    q_row, mode_row = slots_row(source[...]), slots_row(modes[...])
    q_col, mode_col = as_column(q_row), as_column(mode_row)
    owner_col, rank_col, _, _ = slot_places(q_row, q_col)
    spot = jnp.where(owner_col >= 0, owner_col * 8 + rank_col, -8)
    spots = jnp.concatenate([spot, spot + PLACES], axis=0)
    pick = (iota((2 * SLOTS, BOX), 1) == spots).astype(F32).astype(BF16)
    for copy in get_small[2:]:
        copy.wait()
    got = dot(pick, side_by_side(answers[...]))
    got = got[:, :LANES] + got[:, LANES:]
    near = owner_col < 0
    row = jnp.where(near, near_row[...], got[:SLOTS])
    col = jnp.where(near, near_col[...], got[SLOTS:])
    lane = iota((SLOTS, LANES), 1)
    chosen = iota((SLOTS, HALF), 1) == mode_col
    factor = jnp.sum(jnp.where(chosen, real[...], 0.0), axis=1, keepdims=True)
    other = jnp.sum(jnp.where(chosen, imag[...], 0.0), axis=1, keepdims=True)
    signed = jnp.where(lane < HALF, -other, other)
    row = factor * row + signed * turn(row)
    col = factor * col - signed * turn(col)
    for k in range(2):
        at = slice(k * LANES, (k + 1) * LANES)
        put_lines(row[at], col[at], rows, cols, k * LANES)
    lines[...] = lax.rem(iota((1, SLOTS), 1), HALF) * HALF + mode_row
    limit = live_s[0] * HALF
    get_part.wait()
    get_parents.wait()
    put_parents.start()

    def add(i, carry):
        base = pl.multiple_of(i * CHUNK, CHUNK)
        at = pl.ds(base, CHUNK)
        result = part[at, :] + slot_sums(rows, cols, lines, base)
        alive = iota((CHUNK, LANES), 0) + base < limit
        done[at, :] = jnp.where(alive, result, 0.0)
        pltpu.make_async_copy(done.at[at, :], child_out.at[at, :], out_sem.at[1]).start()
        return carry

    lax.fori_loop(0, ROWS // CHUNK, add, 0, unroll=4)
    pltpu.make_async_copy(done, child_out, out_sem.at[1]).wait()
    put_parents.wait()


VMEM = pl.BlockSpec(memory_space=pltpu.VMEM)
SMEM = pl.BlockSpec(memory_space=pltpu.SMEM)
HBM = pl.BlockSpec(memory_space=pltpu.HBM)


def body(
    children, parents, hamiltonian, damping, coupling_real, coupling_imag,
    child_modes, child_source, parent_modes, send_rows, live_count,
):
    modes, source, parent_modes = child_modes.T, child_source.T, parent_modes.T
    lines = jax.ShapeDtypeStruct((SLOTS, LANES), F32)
    box = jax.ShapeDtypeStruct((BOX, LANES), F32)
    whole = jax.ShapeDtypeStruct((ROWS, LANES), F32)
    every = REQS + SLOTS
    answers, near_row, near_col, kids_part, folks_done = pl.pallas_call(
        exchange_kernel,
        out_shape=(box, lines, lines, whole, whole),
        in_specs=[SMEM] * 5 + [HBM] * 6,
        out_specs=(HBM,) * 5,
        scratch_shapes=[pltpu.VMEM((ROWS, LANES), F32)] * 6
        + [pltpu.VMEM((BOX, LANES), F32)] * 3
        + [pltpu.VMEM((SLOTS, LANES), F32)] * 4
        + [
            pltpu.VMEM((4, HALF), I32),
            pltpu.VMEM((4, HALF), I32),
            pltpu.VMEM((2, DEVICES), I32),
            pltpu.VMEM((HALF, HALF), F32),
            pltpu.VMEM((8, LANES), I32),
            pltpu.SMEM((8, LANES), I32),
            pltpu.VMEM((2 * LANES, 2 * LANES), BF16),
            pltpu.VMEM((HALF, 2 * LANES), BF16),
            pltpu.VMEM((every, 2 * LANES), BF16),
            pltpu.VMEM((2 * LANES, every), BF16),
            pltpu.VMEM((1, every), I32),
            pltpu.SemaphoreType.DMA((3,)),
            pltpu.SemaphoreType.DMA((4,)),
            pltpu.SemaphoreType.DMA((4,)),
            pltpu.SemaphoreType.DMA((4,)),
            pltpu.SemaphoreType.DMA((2,)),
            pltpu.SemaphoreType.DMA((2,)),
            pltpu.SemaphoreType.DMA((2,)),
        ],
        compiler_params=pltpu.CompilerParams(
            collective_id=0, has_side_effects=True, vmem_limit_bytes=60 * 2**20
        ),
    )(
        modes, source, parent_modes, live_count, damping, modes, source, send_rows[0].T, hamiltonian,
        children.reshape(ROWS, LANES), parents.reshape(ROWS, LANES),
    )
    child_rates, parent_rates = pl.pallas_call(
        rates_kernel,
        out_shape=(whole, whole),
        in_specs=[SMEM] + [HBM] * 9,
        out_specs=(HBM, HBM),
        scratch_shapes=[
            pltpu.VMEM((ROWS, LANES), F32),
            pltpu.VMEM((ROWS, LANES), F32),
            pltpu.VMEM((ROWS, LANES), F32),
            pltpu.VMEM((BOX, LANES), F32),
            pltpu.VMEM((SLOTS, LANES), F32),
            pltpu.VMEM((SLOTS, LANES), F32),
            pltpu.VMEM((4, HALF), I32),
            pltpu.VMEM((4, HALF), I32),
            pltpu.VMEM((1, HALF), F32),
            pltpu.VMEM((1, HALF), F32),
            pltpu.VMEM((SLOTS, 2 * LANES), BF16),
            pltpu.VMEM((2 * LANES, SLOTS), BF16),
            pltpu.VMEM((1, SLOTS), I32),
            pltpu.SemaphoreType.DMA((2,)),
            pltpu.SemaphoreType.DMA((7,)),
            pltpu.SemaphoreType.DMA((2,)),
        ],
        compiler_params=pltpu.CompilerParams(vmem_limit_bytes=60 * 2**20),
    )(
        live_count, modes, source, coupling_real.reshape(1, HALF), coupling_imag.reshape(1, HALF),
        answers, near_row, near_col, kids_part, folks_done,
    )
    return child_rates.reshape(children.shape), parent_rates.reshape(parents.shape)


def solution(mesh):
    in_specs = (
        P(("lo", "hi"), None, None),
        P(("lo", "hi"), None, None),
        P(),
        P(),
        P(),
        P(),
        P(("lo", "hi"), None),
        P(("lo", "hi"), None),
        P(("lo", "hi"), None),
        P(("lo", "hi"), None, None),
        P(("lo", "hi")),
    )
    out_specs = (P(("lo", "hi"), None, None), P(("lo", "hi"), None, None))
    return jax.shard_map(body, mesh=mesh, in_specs=in_specs, out_specs=out_specs, check_vma=False)
```
